32 devices in a mesh: row: 4 (over y, x), col: 8 (over z, core).
Axes of the slice: x: 2, y: 2, z: 4, core: 2. Of those that a mesh axis runs over, the one named last changes fastest.
Arguments:
- tokens: bfloat16 [128, 257, 1024], P(('row', 'col')), may hold values from -6 to 6
- positions: int32 [128], P(('row', 'col')), may hold values from 0 to 767, as said below
- cached: bfloat16 [768, 1024], P(('row', 'col')), may hold values from -6 to 6
- labels: int32 [8, 768], replicated, may hold values from 0 to 1073741823, as said below
- w_kv: bfloat16 [1024, 2048], P('col', 'row'), may hold values from -1 to 1
- w_query: bfloat16 [1024, 1024], P('col', 'row'), may hold values from -12 to 12
- w_out: bfloat16 [1024, 1024], P('row', 'col'), may hold values from -0.1875 to 0.1875
- norm_gain: float32 [1024], replicated, may hold values from 0.25 to 1.75
- norm_bias: float32 [1024], replicated, may hold values from -3 to 3
- query_bias: float32 [1024], replicated, may hold values from -4 to 4
- value_bias: float32 [1024], replicated, may hold values from -4 to 4
- layer_scale: float32 [1024], replicated, may hold values from 0.5 to 4
- final_gain: float32 [1024], replicated, may hold values from 0.25 to 1.75
- final_bias: float32 [1024], replicated, may hold values from -3 to 3
Outputs:
- proof: float32 [768, 240], P(('row', 'col'))
- statistic: float32 [240], replicated
The draws below stay inside these ranges and needn't reach their ends.
Inputs may be any that keep to these rules, and one draw needn't show every extreme that they name: Image i's position lies among the 24 rows that begin at (i // 4) * 24; different images have different positions. Every permutation labels exactly 384 samples with 1.
All inputs are finite; a program needn't handle non-finite values.
Results may differ from the reference program's by a relative error of at most 0.005.
Values may be sent and summed in bfloat16 or wider, within the bound.
A program may use at most 64 MiB of HBM per device.

```python
import math
import jax
import jax.numpy as jnp
from jax import lax

D = 1024
HEADS = 16
HEAD = 64
TOK = 257
IMG_DEV = 4
IMAGES = 128
ROWS_DEV = 24
M = 768
PERMS = 240
WORDS = 8
N_ROW = 4
DEVICES = 32


def pick_rows(key):
    return jax.random.permutation(key, ROWS_DEV)[:IMG_DEV]


def draw_positions(key, part):
    keys = jax.random.split(jax.random.fold_in(key, 11), DEVICES)
    picks = jax.vmap(pick_rows)(keys).astype(jnp.int32)
    base = jnp.arange(DEVICES, dtype=jnp.int32)[:, None] * ROWS_DEV
    return (picks + base).reshape(IMAGES).astype(jnp.int32)


def label_bits(key):
    return (jax.random.permutation(key, M) < M // 2).astype(jnp.int32)


def draw_labels(key, part):
    keys = jax.random.split(jax.random.fold_in(key, 23), PERMS)
    bits = jax.vmap(label_bits)(keys).reshape(WORDS, 30, M)
    powers = jnp.left_shift(jnp.ones((30,), jnp.int32), jnp.arange(30, dtype=jnp.int32))
    return jnp.sum(bits * powers[None, :, None], axis=1).astype(jnp.int32)


def key_columns(key):
    base = jax.random.normal(jax.random.fold_in(key, 31), (D, HEADS, HEAD), jnp.float32)
    return jnp.clip(base, -6.0, 6.0) * D ** (-0.5)


def draw_w_kv(key, part):
    keys_part = key_columns(key)
    values_raw = jax.random.normal(jax.random.fold_in(key, 37), (D, HEADS, HEAD), jnp.float32)
    values_part = jnp.clip(values_raw, -6.0, 6.0) * D ** (-0.5)
    return jnp.stack([keys_part, values_part], axis=2).reshape(D, 2 * D).astype(jnp.bfloat16)


def draw_w_query(key, part):
    own_raw = jax.random.normal(jax.random.fold_in(key, 41), (D, D), jnp.float32)
    own_part = jnp.clip(own_raw, -6.0, 6.0) * D ** (-0.5)
    return own_part.astype(jnp.bfloat16)


def draw_tokens(key, part):
    base = jax.random.normal(jax.random.fold_in(key, 53), (IMAGES, TOK, D), jnp.float32)
    base = jnp.clip(base, -6.0, 6.0)
    return base.astype(jnp.bfloat16)


def steps_of(own_key, shape, pieces, smallest, largest):
    loudness, own = 1.0, jax.random.fold_in(own_key, 6)
    for dim, blocks in pieces:
        heights = jnp.exp(jax.random.uniform(jax.random.fold_in(own, dim), (blocks,), jnp.float32, smallest / len(pieces), largest / len(pieces)))
        loudness = loudness * jnp.repeat(heights, shape[dim] // blocks).reshape([-1 if axis == dim else 1 for axis in range(len(shape))])
    return loudness


def bell_draw(key, extent, scale, limit, shards=(), kind=jnp.bfloat16):
    factor_of = steps_of(key, extent, shards, -0.22, 0.18) if shards else 1.0
    values = jax.random.normal(key, extent, jnp.float32) * scale * factor_of
    return jnp.minimum(jnp.maximum(values, -limit), limit).astype(kind)


def setup_inputs(seed: int = 0) -> dict:
    arg_keys = jax.random.split(jax.random.key(seed), 15)
    tokens = draw_tokens(jax.random.fold_in(arg_keys[14], 71), 0)
    positions = draw_positions(jax.random.fold_in(arg_keys[14], 71), 0)
    cached = bell_draw(arg_keys[2], (M, D), 1.0, 6.0, ((0, 32),))
    labels = draw_labels(jax.random.fold_in(arg_keys[14], 71), 0)
    w_kv = draw_w_kv(jax.random.fold_in(arg_keys[14], 71), 0)
    w_query = draw_w_query(jax.random.fold_in(arg_keys[14], 71), 0)
    w_out = bell_draw(arg_keys[6], (D, D), D ** -0.5, 0.1875, ((0, 4), (1, 8)))
    norm_gain = jnp.clip(1.0 + 0.15 * jax.random.normal(arg_keys[7], (D,), jnp.float32), 0.25, 1.75)
    norm_bias = bell_draw(arg_keys[8], (D,), 0.5, 3.0, (), jnp.float32)
    query_bias = bell_draw(arg_keys[9], (D,), 1.0, 4.0, (), jnp.float32)
    value_bias = bell_draw(arg_keys[10], (D,), 1.0, 4.0, (), jnp.float32)
    layer_scale = jnp.clip(jnp.exp(jax.random.uniform(arg_keys[11], (D,), jnp.float32, math.log(0.5), math.log(4.0))), 0.5, 4.0)
    final_gain = jnp.clip(1.0 + 0.15 * jax.random.normal(arg_keys[12], (D,), jnp.float32), 0.25, 1.75)
    final_bias = bell_draw(arg_keys[13], (D,), 0.5, 3.0, (), jnp.float32)
    return {"tokens": tokens, "positions": positions, "cached": cached, "labels": labels, "w_kv": w_kv, "w_query": w_query, "w_out": w_out, "norm_gain": norm_gain, "norm_bias": norm_bias, "query_bias": query_bias, "value_bias": value_bias, "layer_scale": layer_scale, "final_gain": final_gain, "final_bias": final_bias}


def layer_norm(values, gain, shift):
    center = values - lax.optimization_barrier(jnp.mean(values, axis=-1, keepdims=True))
    spread = lax.optimization_barrier(jnp.mean(center * center, axis=-1, keepdims=True))
    return center * lax.rsqrt(spread + 1e-06) * gain + shift

def unpack_signs(words):
    shifts = jnp.arange(30, dtype=jnp.int32)
    bits = jnp.bitwise_and(jnp.right_shift(words[:, None, :], shifts[None, :, None]), 1)
    bits = bits.reshape(PERMS, words.shape[1])
    return (2 * bits - 1).astype(jnp.float32).T

def reference(tokens, positions, cached, labels, w_kv, w_query, w_out, norm_gain, norm_bias, query_bias, value_bias, layer_scale, final_gain, final_bias):
    highest = lax.Precision.HIGHEST
    pair_weight = w_kv.reshape(D, HEADS, 2, HEAD)
    key_weight = pair_weight[:, :, 0].astype(jnp.float32)
    value_weight = pair_weight[:, :, 1].astype(jnp.float32)

    def embed_image(image):
        as_float = image.astype(jnp.float32)
        normed = layer_norm(as_float, norm_gain, norm_bias).astype(jnp.bfloat16)
        query = jnp.dot(normed[0], w_query, preferred_element_type=jnp.float32) + query_bias
        query = query.reshape(HEADS, HEAD) * HEAD ** (-0.5)
        folded = jnp.einsum('dhe,he->dh', key_weight, query, precision=highest)
        normed_float = normed.astype(jnp.float32)
        scores = jnp.dot(normed_float, folded, precision=highest)
        top = lax.optimization_barrier(jnp.max(scores, axis=0, keepdims=True))
        expo = jnp.exp(scores - top)
        attend = expo / lax.optimization_barrier(jnp.sum(expo, axis=0, keepdims=True))
        pooled_heads = jnp.einsum('th,td->hd', attend, normed_float, precision=highest)
        mixed = jnp.einsum('hd,dhe->he', pooled_heads, value_weight, precision=highest).reshape(D) + value_bias
        projected = jnp.dot(mixed.astype(jnp.bfloat16), w_out, preferred_element_type=jnp.float32)
        residual_sum = as_float[0] + layer_scale * projected
        return layer_norm(residual_sum, final_gain, final_bias).astype(jnp.bfloat16)
    embedding = lax.map(embed_image, tokens)
    pooled = cached.at[positions].set(embedding)
    signs = unpack_signs(labels)
    block_rows = M // N_ROW

    def kernel_block(first_row):
        picked = lax.dynamic_slice_in_dim(pooled, first_row, block_rows, 0)
        inner = jnp.einsum('rd,cd->rc', picked, pooled, preferred_element_type=jnp.float32)
        kernel = (inner / D + 1.0) ** 3
        product = jnp.dot(kernel, signs, precision=highest)
        row_signs = lax.dynamic_slice_in_dim(signs, first_row, block_rows, 0)
        return (product, lax.optimization_barrier(jnp.sum(row_signs * product, axis=0)))
    starts = (jnp.arange(N_ROW) * block_rows).astype(jnp.int32)
    product, quad = lax.map(kernel_block, starts)
    own_square = jnp.einsum('rd,rd->r', pooled, pooled, preferred_element_type=jnp.float32)
    trace = jnp.sum((own_square / D + 1.0) ** 3)
    proof = product.reshape(M, PERMS) * M ** (-0.5)
    statistic = (lax.optimization_barrier(jnp.sum(quad, axis=0)) - trace) / M
    return (proof, statistic)
```

```python
import functools
import jax
import jax.numpy as jnp
from jax import lax
from jax.experimental import pallas as pl
from jax.experimental.pallas import tpu as pltpu
from jax.sharding import PartitionSpec as P

HEADS = 16
PERMS = 240
LANES = 256
SLOT = 32
F32 = jnp.float32
BF16 = jnp.bfloat16
NT = (((1,), (1,)), ((), ()))


def layer_norm(values, gain, shift):
    center = values - jnp.mean(values, axis=-1, keepdims=True)
    spread = jnp.mean(center * center, axis=-1, keepdims=True)
    return center * lax.rsqrt(spread + 1e-06) * gain + shift


def pieces(values, count=3):
    parts = []
    for _ in range(count):
        part = values.astype(BF16)
        parts.append(part)
        values = values - part.astype(F32)
    return jnp.concatenate(parts, axis=0)


def fold_pieces(values, count=3):
    rows = values.shape[0] // count
    total = values[:rows]
    for step in range(1, count):
        total = total + values[step * rows : (step + 1) * rows]
    return total


def kernel_body(
    R, C, images, tok, D, rows_dev,
    tokens, positions, cached, wq, wkv, wo,
    gain, shift, qbias, vbias, scale, fgain, fshift, row_signs, col_signs,
    proof, stat,
    normed, cls, wq_g, wkv_g, wo_g,
    a_row, a_col, pos_row, pos_col, fold_s, fold_r, pool_s, pool_r, proj_s, proj_r,
    e_row, e_col, part, part_r, quad_c, quad_r,
    s_cls, r_cls, s_w, r_w, s_cach, r_cach_row, r_cach_col, r_pos_row, r_pos_col,
    s_fold, r_fold, s_pool, r_pool, s_proj, r_proj, s_emb, r_emb_row, r_emb_col,
    s_part, r_part, s_qc, r_qc, s_qr, r_qr,
):
    r = lax.axis_index("row")
    c = lax.axis_index("col")
    HR = HEADS // R
    head = D // HEADS
    half = C // 2
    core = lax.rem(c, 2)
    sib = c + 1 - 2 * core
    row_peers = [lax.rem(r + t, R) for t in range(1, R)]
    col_peers = [lax.rem(c + t, C) for t in range(1, C)]
    chip_peers = [core + 2 * lax.rem(c // 2 + t, half) for t in range(1, half)]
    sent = []

    def send(src, dst, ssem, rsem, dev):
        copy = pltpu.make_async_remote_copy(
            src_ref=src, dst_ref=dst, send_sem=ssem, recv_sem=rsem,
            device_id=dev, device_id_type=pl.DeviceIdType.MESH,
        )
        copy.start()
        sent.append(copy)

    def arrive(dst, ssem, rsem):
        pltpu.make_async_remote_copy(
            src_ref=dst, dst_ref=dst, send_sem=ssem, recv_sem=rsem,
            device_id=(r, sib), device_id_type=pl.DeviceIdType.MESH,
        ).wait_recv()

    barrier = pltpu.get_barrier_semaphore()
    for rr in row_peers:
        pl.semaphore_signal(barrier, inc=1, device_id=(rr, c), device_id_type=pl.DeviceIdType.MESH)
    for cc in col_peers:
        pl.semaphore_signal(barrier, inc=1, device_id=(r, cc), device_id_type=pl.DeviceIdType.MESH)

    wrows = D // C

    def wslot(ref, index):
        return ref.at[pl.ds(pl.multiple_of(index * wrows, wrows), wrows)]

    cls[r] = jnp.zeros(cls.shape[1:], F32)
    for i in range(images):
        cls[r, i : i + 1, :] = tokens[i, 0:16, :].astype(F32)[0:1]
    weights = ((wq, wq_g), (wkv, wkv_g), (wo, wo_g))
    for own, full in weights:
        wslot(full, c)[...] = own[...]
    first_row = (r * C + c) * rows_dev
    local = [(positions[i] - first_row).astype(F32) for i in range(images)]
    sub = lax.broadcasted_iota(jnp.int32, (rows_dev, 1), 0).astype(F32)
    hit = jnp.zeros((rows_dev, 1), F32)
    for value in local:
        hit = jnp.where(sub == value, 1.0, hit)
    kept = cached[...].astype(F32) * (1.0 - hit)
    kept = jnp.concatenate([kept, jnp.zeros((SLOT - rows_dev, D), F32)], axis=0).astype(BF16)
    a_row[c] = kept
    a_col[r] = kept
    lane4 = lax.rem(lax.broadcasted_iota(jnp.int32, pos_row.shape[1:], 1), images)
    tile = jnp.zeros(pos_row.shape[1:], F32)
    for i in range(images):
        tile = jnp.where(lane4 == i, local[i], tile)
    pos_row[c] = tile
    pos_col[r] = tile

    pl.semaphore_wait(barrier, R - 1 + C - 1)

    for t, rr in enumerate(row_peers):
        send(cls.at[r], cls.at[r], s_cls.at[t], r_cls.at[r], (rr, c))
    for w, (own, full) in enumerate(weights):
        for t, cc in enumerate(chip_peers + [sib]):
            send(wslot(full, c), wslot(full, c), s_w.at[w, t], r_w.at[w, c], (r, cc))
    for t, rr in enumerate(row_peers):
        send(a_col.at[r], a_col.at[r], s_cach.at[0, t], r_cach_col.at[r], (rr, c))
        send(pos_col.at[r], pos_col.at[r], s_cach.at[1, t], r_pos_col.at[r], (rr, c))
    for t, cc in enumerate(col_peers):
        send(a_row.at[c], a_row.at[c], s_cach.at[2, t], r_cach_row.at[c], (r, cc))
        send(pos_row.at[c], pos_row.at[c], s_cach.at[3, t], r_pos_row.at[c], (r, cc))

    def forward(w):
        full = weights[w][1]
        for t, cc in enumerate(chip_peers):
            arrive(wslot(full, cc), s_w.at[w, 0], r_w.at[w, cc])
            send(wslot(full, cc), wslot(full, cc), s_w.at[w, half + t], r_w.at[w, cc], (r, sib))

    def complete(w):
        full = weights[w][1]
        arrive(wslot(full, sib), s_w.at[w, 0], r_w.at[w, sib])
        for cc in chip_peers:
            other = cc + 1 - 2 * core
            arrive(wslot(full, other), s_w.at[w, 0], r_w.at[w, other])

    for i in range(images):
        @pl.loop(0, tok // 32)
        def _(j):
            at = pl.ds(pl.multiple_of(j * 32, 32), 32)
            normed[i, at, :] = layer_norm(tokens[i, at, :].astype(F32), gain[...], shift[...]).astype(BF16)
        last = (tok // 32) * 32
        if last < tok:
            normed[i, last:tok, :] = layer_norm(
                tokens[i, last:tok, :].astype(F32), gain[...], shift[...]
            ).astype(BF16)

    for rr in row_peers:
        arrive(cls.at[rr], s_cls.at[0], r_cls.at[rr])
    group = jnp.concatenate([cls[j, 0:images, :] for j in range(R)], axis=0)
    normed0 = layer_norm(group, gain[...], shift[...]).astype(BF16)

    forward(0)
    complete(0)
    query = jnp.dot(normed0, wq_g[...], preferred_element_type=F32) + qbias[pl.ds(r, 1), :]
    query = query * head ** (-0.5)
    forward(1)
    complete(1)
    count = R * images
    for h in range(HR):
        own = query[:, h * head : (h + 1) * head]
        own = jnp.concatenate([own, jnp.zeros((count, head), F32)], axis=1)
        folded = lax.dot_general(
            pieces(own), wkv_g[:, 2 * h * head : 2 * (h + 1) * head], NT, preferred_element_type=F32
        )
        folded = fold_pieces(folded)
        for j in range(R):
            fold_s[j, h * images : (h + 1) * images, :] = folded[j * images : (j + 1) * images]
    for t, rr in enumerate(row_peers):
        send(fold_s.at[rr], fold_r.at[r], s_fold.at[t], r_fold.at[r], (rr, c))
    fold_r[r] = fold_s[r]
    forward(2)
    for rr in row_peers:
        arrive(fold_r.at[rr], s_fold.at[0], r_fold.at[rr])

    for i in range(images):
        mine = jnp.concatenate(
            [fold_r[j, h * images + i : h * images + i + 1, :] for j in range(R) for h in range(HR)], axis=0
        )
        scores = fold_pieces(
            lax.dot_general(pieces(mine), normed[i], NT, preferred_element_type=F32)
        )
        expo = jnp.exp(scores - jnp.max(scores, axis=-1, keepdims=True))
        attend = expo / jnp.sum(expo, axis=-1, keepdims=True)
        pooled = fold_pieces(jnp.dot(pieces(attend), normed[i], preferred_element_type=F32))
        for j in range(R):
            pool_s[j, i * HR : (i + 1) * HR, :] = pooled[j * HR : (j + 1) * HR]
    for t, rr in enumerate(row_peers):
        send(pool_s.at[rr], pool_r.at[r], s_pool.at[t], r_pool.at[r], (rr, c))
    pool_r[r] = pool_s[r]
    complete(2)
    for rr in row_peers:
        arrive(pool_r.at[rr], s_pool.at[0], r_pool.at[rr])

    heads = []
    for h in range(HR):
        mine = jnp.concatenate(
            [pool_r[j, i * HR + h : i * HR + h + 1, :] for j in range(R) for i in range(images)], axis=0
        )
        got = fold_pieces(
            jnp.dot(pieces(mine), wkv_g[:, 2 * h * head : 2 * (h + 1) * head], preferred_element_type=F32)
        )
        heads.append(got[:, head : 2 * head])
    mixed = jnp.concatenate(heads, axis=1) if HR > 1 else heads[0]
    mixed = (mixed + vbias[pl.ds(r, 1), :]).astype(BF16)
    projected = lax.dot_general(mixed, wo_g[...], NT, preferred_element_type=F32)
    for j in range(R):
        proj_s[j] = projected[j * images : (j + 1) * images]
    for t, rr in enumerate(row_peers):
        send(proj_s.at[rr], proj_r.at[r], s_proj.at[t], r_proj.at[r], (rr, c))
    proj_r[r] = proj_s[r]
    for rr in row_peers:
        arrive(proj_r.at[rr], s_proj.at[0], r_proj.at[rr])
    total = proj_r[0]
    for j in range(1, R):
        total = total + proj_r[j]
    residual = cls[r, 0:images, :] + scale[...] * total
    embedding = layer_norm(residual, fgain[...], fshift[...])
    folds = 16 // images
    wide = D // folds
    packed = jnp.concatenate([embedding[:, s * wide : (s + 1) * wide] for s in range(folds)], axis=0)
    e_row[c] = packed.astype(BF16)
    e_col[r] = packed.astype(BF16)
    for t, cc in enumerate(col_peers):
        send(e_row.at[c], e_row.at[c], s_emb.at[1, t], r_emb_row.at[c], (r, cc))
    for t, rr in enumerate(row_peers):
        send(e_col.at[r], e_col.at[r], s_emb.at[0, t], r_emb_col.at[r], (rr, c))

    for rr in row_peers:
        arrive(a_col.at[rr], s_cls.at[0], r_cach_col.at[rr])
        arrive(pos_col.at[rr], s_cls.at[0], r_pos_col.at[rr])
    for cc in col_peers:
        arrive(a_row.at[cc], s_cls.at[0], r_cach_row.at[cc])
        arrive(pos_row.at[cc], s_cls.at[0], r_pos_row.at[cc])

    def pick(pos, blocks, s):
        shape = (blocks * SLOT, blocks * 16)
        a = lax.broadcasted_iota(jnp.int32, shape, 0)
        b = lax.broadcasted_iota(jnp.int32, shape, 1)
        same = (a // SLOT == b // 16) & (lax.rem(b, 16) // images == s)
        stacked = jnp.concatenate(
            [jnp.broadcast_to(pos[j, 0:1, 0 : blocks * 16], (SLOT, blocks * 16)) for j in range(blocks)], axis=0
        )
        return jnp.where(same & (lax.rem(a, SLOT).astype(F32) == stacked), 1.0, 0.0).astype(BF16)

    def merged(kept_ref, pos, emb, blocks):
        base = kept_ref[...].reshape(blocks * SLOT, D)
        flat = emb[...].reshape(blocks * 16, wide)
        outs = []
        for s in range(folds):
            moved = jnp.dot(pick(pos, blocks, s), flat, preferred_element_type=F32)
            outs.append((base[:, s * wide : (s + 1) * wide].astype(F32) + moved).astype(BF16))
        return jnp.concatenate(outs, axis=1)

    for rr in row_peers:
        arrive(e_col.at[rr], s_cls.at[0], r_emb_col.at[rr])
    for cc in col_peers:
        arrive(e_row.at[cc], s_cls.at[0], r_emb_row.at[cc])
    rows = merged(a_row, pos_row, e_row, C)
    cols = merged(a_col, pos_col, e_col, R)
    inner = lax.dot_general(rows, cols, NT, preferred_element_type=F32)
    base = inner / D + 1.0
    gram = base * base * base
    ga = lax.broadcasted_iota(jnp.int32, gram.shape, 0) - SLOT * c
    gb = lax.broadcasted_iota(jnp.int32, gram.shape, 1) - SLOT * r
    diagonal = (ga == gb) & (ga >= 0) & (ga < rows_dev)
    trace = jnp.sum(jnp.where(diagonal, gram, 0.0))
    product = fold_pieces(jnp.dot(pieces(gram), col_signs[...], preferred_element_type=F32))
    for j in range(C):
        part[j] = product[j * SLOT : j * SLOT + rows_dev]
    for t, cc in enumerate(col_peers):
        send(part.at[cc], part_r.at[c], s_part.at[t], r_part.at[c], (r, cc))
    quad = jnp.sum(row_signs[...] * product, axis=0, keepdims=True) - trace
    quad_c[c] = jnp.broadcast_to(quad, (8, LANES))
    for t, cc in enumerate(col_peers):
        send(quad_c.at[c], quad_c.at[c], s_qc.at[t], r_qc.at[c], (r, cc))
    part_r[c] = part[c]
    for cc in col_peers:
        arrive(quad_c.at[cc], s_cls.at[0], r_qc.at[cc])
    total = quad_c[0]
    for j in range(1, C):
        total = total + quad_c[j]
    quad_r[r] = total
    for t, rr in enumerate(row_peers):
        send(quad_r.at[r], quad_r.at[r], s_qr.at[t], r_qr.at[r], (rr, c))
    for cc in col_peers:
        arrive(part_r.at[cc], s_cls.at[0], r_part.at[cc])
    summed = part_r[0]
    for j in range(1, C):
        summed = summed + part_r[j]
    samples = rows_dev * R * C
    proof[...] = (summed * samples ** (-0.5))[:, 0:PERMS]
    for rr in row_peers:
        arrive(quad_r.at[rr], s_cls.at[0], r_qr.at[rr])
    total = quad_r[0]
    for j in range(1, R):
        total = total + quad_r[j]
    stat[...] = (total[0:1, :] / samples)[:, 0:PERMS]
    for copy in sent:
        copy.wait_send()


def unpack(words, blocks, rows_dev):
    shifts = jnp.arange(30, dtype=jnp.int32)
    bits = jnp.bitwise_and(jnp.right_shift(words[:, None, :], shifts[None, :, None]), 1)
    signs = (2 * bits - 1).reshape(PERMS, blocks, rows_dev)
    signs = jnp.pad(signs, ((0, LANES - PERMS), (0, 0), (0, SLOT - rows_dev)))
    return signs.reshape(LANES, blocks * SLOT).T


def per_device(
    R, C, tokens, positions, cached, labels, w_kv, w_query, w_out,
    norm_gain, norm_bias, query_bias, value_bias, layer_scale, final_gain, final_bias,
):
    images, tok, D = tokens.shape
    rows_dev = cached.shape[0]
    HR = HEADS // R
    row_index = lax.axis_index("row")
    col_index = lax.axis_index("col")
    words = labels.shape[0]
    row_words = lax.dynamic_slice_in_dim(labels, row_index * (rows_dev * C), rows_dev * C, 1)
    col_words = lax.dynamic_slice_in_dim(
        labels.reshape(words, R, C, rows_dev), col_index, 1, 2
    ).reshape(words, R * rows_dev)
    row_signs = unpack(row_words, C, rows_dev).astype(F32)
    col_signs = unpack(col_words, R, rows_dev).astype(BF16)
    flat = lambda v: v.reshape(1, D)
    by_row = lambda v: v.reshape(R, D // R)
    vm = pl.BlockSpec(memory_space=pltpu.VMEM)
    sm = pl.BlockSpec(memory_space=pltpu.SMEM)
    V = pltpu.VMEM
    S = lambda *shape: pltpu.SemaphoreType.DMA(shape)
    wide = max(128, 16 * R, 16 * C)
    scratch = [
        V((images, tok, D), BF16), V((R, 8, D), F32),
        V((D, w_query.shape[1]), BF16), V((D, w_kv.shape[1]), BF16), V((D, w_out.shape[0]), BF16),
        V((C, SLOT, D), BF16), V((R, SLOT, D), BF16), V((C, 8, wide), F32), V((R, 8, wide), F32),
        V((R, HR * images, D), F32), V((R, HR * images, D), F32),
        V((R, HR * images, D), F32), V((R, HR * images, D), F32),
        V((R, images, D), F32), V((R, images, D), F32),
        V((C, 16, D * images // 16), BF16), V((R, 16, D * images // 16), BF16),
        V((C, rows_dev, LANES), F32), V((C, rows_dev, LANES), F32),
        V((C, 8, LANES), F32), V((R, 8, LANES), F32),
        S(R), S(R), S(3, C), S(3, C), S(4, max(R, C)), S(C), S(R), S(C), S(R),
        S(R), S(R), S(R), S(R), S(R), S(R), S(2, max(R, C)), S(C), S(R),
        S(C), S(C), S(C), S(C), S(R), S(R),
    ]
    proof, stat = pl.pallas_call(
        functools.partial(kernel_body, R, C, images, tok, D, rows_dev),
        out_shape=(
            jax.ShapeDtypeStruct((rows_dev, PERMS), F32),
            jax.ShapeDtypeStruct((1, PERMS), F32),
        ),
        in_specs=[vm, sm] + [vm] * 13,
        out_specs=(vm, vm),
        scratch_shapes=scratch,
        compiler_params=pltpu.CompilerParams(
            collective_id=0, has_side_effects=True, vmem_limit_bytes=48 * 1024 * 1024
        ),
    )(
        tokens, positions, cached, w_query, w_kv, w_out.T,
        flat(norm_gain), flat(norm_bias), by_row(query_bias), by_row(value_bias), flat(layer_scale),
        flat(final_gain), flat(final_bias), row_signs, col_signs,
    )
    return proof, stat.reshape(PERMS)


def solution(mesh):
    placed = (
        P(("row", "col"), None, None),
        P(("row", "col")),
        P(("row", "col"), None),
        P(),
        P("col", "row"),
        P("col", "row"),
        P("row", "col"),
        P(), P(), P(), P(), P(), P(), P(),
    )
    return jax.shard_map(
        functools.partial(per_device, mesh.shape["row"], mesh.shape["col"]),
        mesh=mesh,
        in_specs=placed,
        out_specs=(P(("row", "col"), None), P()),
        check_vma=False,
    )
```

```python
import functools
import jax
import jax.numpy as jnp
from jax import lax
from jax.experimental import pallas as pl
from jax.experimental.pallas import tpu as pltpu
from jax.sharding import PartitionSpec as P

HEADS = 16
PERMS = 240
LANES = 256
SLOT = 32
F32 = jnp.float32
BF16 = jnp.bfloat16
NT = (((1,), (1,)), ((), ()))


def layer_norm(values, gain, shift):
    center = values - jnp.mean(values, axis=-1, keepdims=True)
    spread = jnp.mean(center * center, axis=-1, keepdims=True)
    return center * lax.rsqrt(spread + 1e-06) * gain + shift


def pieces(values, count=3):
    parts = []
    for _ in range(count):
        part = values.astype(BF16)
        parts.append(part)
        values = values - part.astype(F32)
    return jnp.concatenate(parts, axis=0)


def fold_pieces(values, count=3):
    rows = values.shape[0] // count
    total = values[:rows]
    for step in range(1, count):
        total = total + values[step * rows : (step + 1) * rows]
    return total


def kernel_body(
    R, C, images, tok, D, rows_dev,
    tokens_hbm, positions, cached, wq, wkv, wo,
    gain, shift, qbias, vbias, scale, fgain, fshift, labels,
    proof, stat,
    tokens, heads16, d_tok, normed, cls, wq_g, wk_g, wv_g, wo_g, row_signs, col_signs, sel_row, sel_col,
    a_row, a_col, pos_row, pos_col, fold_s, fold_r, pool_s, pool_r, proj_s, proj_r,
    e_row, e_col, part, part_r, quad_c, quad_r,
    s_cls, r_cls, s_w, r_w, s_cach, r_cach_row, r_cach_col, r_pos_row, r_pos_col,
    s_fold, r_fold, s_pool, r_pool, s_proj, r_proj, s_emb, r_emb_row, r_emb_col,
    s_part, r_part, s_qc, r_qc, s_qr, r_qr,
):
    r = lax.axis_index("row")
    c = lax.axis_index("col")
    HR = HEADS // R
    head = D // HEADS
    half = C // 2
    core = lax.rem(c, 2)
    sib = c + 1 - 2 * core
    row_peers = [lax.rem(r + t, R) for t in range(1, R)]
    col_peers = [lax.rem(c + t, C) for t in range(1, C)]
    chip_peers = [core + 2 * lax.rem(c // 2 + t, half) for t in range(1, half)]
    sent = []

    def send(src, dst, ssem, rsem, dev):
        copy = pltpu.make_async_remote_copy(
            src_ref=src, dst_ref=dst, send_sem=ssem, recv_sem=rsem,
            device_id=dev, device_id_type=pl.DeviceIdType.MESH,
        )
        copy.start()
        sent.append(copy)

    def arrive(dst, ssem, rsem):
        pltpu.make_async_remote_copy(
            src_ref=dst, dst_ref=dst, send_sem=ssem, recv_sem=rsem,
            device_id=(r, sib), device_id_type=pl.DeviceIdType.MESH,
        ).wait_recv()

    head_copy = pltpu.make_async_copy(tokens_hbm.at[:, pl.ds(0, 16), :], heads16, d_tok.at[images])
    head_copy.start()
    loads = [pltpu.make_async_copy(tokens_hbm.at[i], tokens.at[i], d_tok.at[i]) for i in range(images)]
    for load in loads:
        load.start()
    barrier = pltpu.get_barrier_semaphore()
    for rr in row_peers:
        pl.semaphore_signal(barrier, inc=1, device_id=(rr, c), device_id_type=pl.DeviceIdType.MESH)
    for cc in col_peers:
        pl.semaphore_signal(barrier, inc=1, device_id=(r, cc), device_id_type=pl.DeviceIdType.MESH)

    wrows = D // C

    def wslot(ref, index):
        return ref.at[pl.ds(pl.multiple_of(index * wrows, wrows), wrows)]

    head_copy.wait()
    cls[r] = jnp.zeros(cls.shape[1:], F32)
    for i in range(images):
        cls[r, i : i + 1, :] = heads16[i].astype(F32)[0:1]
    weights = (wq_g, wk_g, wv_g, wo_g)
    both = [wkv[:, s * head : (s + 1) * head] for s in range(2 * HR)]
    wslot(wq_g, c)[...] = wq[...]
    wslot(wk_g, c)[...] = jnp.concatenate(both[0::2], axis=1)
    wslot(wv_g, c)[...] = jnp.concatenate(both[1::2], axis=1)
    wslot(wo_g, c)[...] = wo[...].astype(F32).T.astype(BF16)
    pl.semaphore_wait(barrier, R - 1 + C - 1)

    for t, rr in enumerate(row_peers):
        send(cls.at[r], cls.at[r], s_cls.at[t], r_cls.at[r], (rr, c))
    for w, full in enumerate(weights):
        for t, cc in enumerate(chip_peers + [sib]):
            send(wslot(full, c), wslot(full, c), s_w.at[w, t], r_w.at[w, c], (r, cc))
    first_row = (r * C + c) * rows_dev
    local = [(positions[i] - first_row).astype(F32) for i in range(images)]
    sub = lax.broadcasted_iota(jnp.int32, (rows_dev, 1), 0).astype(F32)
    hit = jnp.zeros((rows_dev, 1), F32)
    for value in local:
        hit = jnp.where(sub == value, 1.0, hit)
    kept = cached[...].astype(F32) * (1.0 - hit)
    kept = jnp.concatenate([kept, jnp.zeros((SLOT - rows_dev, D), F32)], axis=0).astype(BF16)
    a_row[c] = kept
    a_col[r] = kept
    lane4 = lax.rem(lax.broadcasted_iota(jnp.int32, pos_row.shape[1:], 1), images)
    tile = jnp.zeros(pos_row.shape[1:], F32)
    for i in range(images):
        tile = jnp.where(lane4 == i, local[i], tile)
    pos_row[c] = tile
    pos_col[r] = tile

    def forward(w):
        full = weights[w]
        for t, cc in enumerate(chip_peers):
            arrive(wslot(full, cc), s_w.at[w, 0], r_w.at[w, cc])
            send(wslot(full, cc), wslot(full, cc), s_w.at[w, half + t], r_w.at[w, cc], (r, sib))

    def complete(w):
        full = weights[w]
        arrive(wslot(full, sib), s_w.at[w, 0], r_w.at[w, sib])
        for cc in chip_peers:
            other = cc + 1 - 2 * core
            arrive(wslot(full, other), s_w.at[w, 0], r_w.at[w, other])

    def share():
        for t, rr in enumerate(row_peers):
            send(a_col.at[r], a_col.at[r], s_cach.at[0, t], r_cach_col.at[r], (rr, c))
            send(pos_col.at[r], pos_col.at[r], s_cach.at[1, t], r_pos_col.at[r], (rr, c))
        for t, cc in enumerate(chip_peers + [sib]):
            send(a_row.at[c], a_row.at[c], s_cach.at[2, t], r_cach_row.at[c], (r, cc))
        for t, cc in enumerate(col_peers):
            send(pos_row.at[c], pos_row.at[c], s_cach.at[3, t], r_pos_row.at[c], (r, cc))

    def share_on():
        for t, cc in enumerate(chip_peers):
            arrive(a_row.at[cc], s_cls.at[0], r_cach_row.at[cc])
            send(a_row.at[cc], a_row.at[cc], s_cach.at[2, half + t], r_cach_row.at[cc], (r, sib))

    def norm_image(i):
        loads[i].wait()

        @pl.loop(0, tok // 32, unroll=2)
        def _(j):
            at = pl.ds(pl.multiple_of(j * 32, 32), 32)
            normed[i, at, :] = layer_norm(tokens[i, at, :].astype(F32), gain[...], shift[...]).astype(BF16)
        last = (tok // 32) * 32
        if last < tok:
            normed[i, last:tok, :] = layer_norm(
                tokens[i, last:tok, :].astype(F32), gain[...], shift[...]
            ).astype(BF16)

    for i in range(images // 2):
        norm_image(i)
    forward(0)
    for i in range(images // 2, images):
        norm_image(i)

    for rr in row_peers:
        arrive(cls.at[rr], s_cls.at[0], r_cls.at[rr])
    group = jnp.concatenate([cls[j, 0:images, :] for j in range(R)], axis=0)
    normed0 = layer_norm(group, gain[...], shift[...]).astype(BF16)

    def own_part(ref):
        size = D // R
        part = ref[:, 0:size]
        for j in range(1, R):
            part = jnp.where(r == j, ref[:, j * size : (j + 1) * size], part)
        return part

    complete(0)
    query = jnp.dot(normed0, wq_g[...], preferred_element_type=F32) + own_part(qbias)
    query = query * head ** (-0.5)
    count = R * images
    of_head = lax.broadcasted_iota(jnp.int32, query.shape, 1) // head
    spread = jnp.concatenate([jnp.where(of_head == h, query, 0.0) for h in range(HR)], axis=0)
    spread = pieces(spread)
    forward(1)
    complete(1)
    folded = fold_pieces(lax.dot_general(spread, wk_g[...], NT, preferred_element_type=F32))
    for h in range(HR):
        for j in range(R):
            at = h * count + j * images
            fold_s[j, h * images : (h + 1) * images, :] = folded[at : at + images]
    for t, rr in enumerate(row_peers):
        send(fold_s.at[rr], fold_r.at[r], s_fold.at[t], r_fold.at[r], (rr, c))
    fold_r[r] = fold_s[r]
    forward(2)
    share()
    samples = rows_dev * R * C
    step = min(samples, 768)

    def chosen(count, first):
        a = lax.broadcasted_iota(jnp.int32, (count * SLOT, step), 0)
        m = lax.broadcasted_iota(jnp.int32, (count * SLOT, step), 1)
        return a // SLOT, lax.rem(a, SLOT), m + first

    row_signs[...] = jnp.zeros(row_signs.shape, F32)
    col_signs[...] = jnp.zeros(col_signs.shape, F32)

    @pl.loop(0, samples // step)
    def _(turn):
        first = pl.multiple_of(turn * step, step)
        perm = lax.broadcasted_iota(jnp.int32, (LANES, step), 0)
        word = jnp.zeros((LANES, step), jnp.int32)
        for w in range(labels.shape[0]):
            word = jnp.where(perm // 30 == w, labels[w : w + 1, pl.ds(first, step)], word)
        bits = jnp.bitwise_and(jnp.right_shift(word, lax.rem(perm, 30)), 1)
        signs = jnp.where(perm < PERMS, 2 * bits - 1, 0).astype(F32).astype(BF16)
        block, inside, m = chosen(C, first)
        one = (m == (r * C + block) * rows_dev + inside) & (inside < rows_dev)
        one = jnp.where(one, 1.0, 0.0).astype(BF16)
        row_signs[...] += lax.dot_general(one, signs, NT, preferred_element_type=F32)
        block, inside, m = chosen(R, first)
        one = (m == (block * C + c) * rows_dev + inside) & (inside < rows_dev)
        one = jnp.where(one, 1.0, 0.0).astype(BF16)
        col_signs[...] += lax.dot_general(one, signs, NT, preferred_element_type=F32)

    for rr in row_peers:
        arrive(fold_r.at[rr], s_fold.at[0], r_fold.at[rr])
    forward(3)

    scores = []
    for i in range(images):
        mine = jnp.concatenate(
            [fold_r[j, h * images + i : h * images + i + 1, :] for j in range(R) for h in range(HR)], axis=0
        )
        scores.append(
            fold_pieces(lax.dot_general(pieces(mine), normed[i], NT, preferred_element_type=F32))
        )
    scores = jnp.concatenate(scores, axis=0)
    expo = jnp.exp(scores - jnp.max(scores, axis=-1, keepdims=True))
    attend = expo / jnp.sum(expo, axis=-1, keepdims=True)
    for i in range(images):
        weight = pieces(attend[i * HEADS : (i + 1) * HEADS])
        pooled = fold_pieces(jnp.dot(weight, normed[i], preferred_element_type=F32))
        for j in range(R):
            for h in range(HR):
                at = h * images + i
                pool_s[j, at : at + 1, :] = pooled[j * HR + h : j * HR + h + 1]
    for t, rr in enumerate(row_peers):
        send(pool_s.at[rr], pool_r.at[r], s_pool.at[t], r_pool.at[r], (rr, c))
    pool_r[r] = pool_s[r]
    complete(2)
    complete(3)
    share_on()
    for rr in row_peers:
        arrive(pool_r.at[rr], s_pool.at[0], r_pool.at[rr])

    mine = jnp.concatenate(
        [pool_r[j, h * images : (h + 1) * images, :] for h in range(HR) for j in range(R)], axis=0
    )
    got = fold_pieces(jnp.dot(pieces(mine), wv_g[...], preferred_element_type=F32))
    mixed = jnp.where(of_head == 0, got[0:count], 0.0)
    for h in range(1, HR):
        mixed = jnp.where(of_head == h, got[h * count : (h + 1) * count], mixed)
    mixed = (mixed + own_part(vbias)).astype(BF16)
    projected = lax.dot_general(mixed, wo_g[...], NT, preferred_element_type=F32)
    for j in range(R):
        proj_s[j] = projected[j * images : (j + 1) * images]
    for t, rr in enumerate(row_peers):
        send(proj_s.at[rr], proj_r.at[r], s_proj.at[t], r_proj.at[r], (rr, c))
    proj_r[r] = proj_s[r]

    folds = 16 // images
    wide = D // folds
    for rr in row_peers:
        arrive(a_col.at[rr], s_cls.at[0], r_cach_col.at[rr])
        arrive(pos_col.at[rr], s_cls.at[0], r_pos_col.at[rr])
    for cc in col_peers:
        arrive(pos_row.at[cc], s_cls.at[0], r_pos_row.at[cc])
    for cc in [sib] + [cc + 1 - 2 * core for cc in chip_peers]:
        arrive(a_row.at[cc], s_cls.at[0], r_cach_row.at[cc])

    def pick(pos, blocks, s):
        shape = (blocks * SLOT, blocks * 16)
        a = lax.broadcasted_iota(jnp.int32, shape, 0)
        b = lax.broadcasted_iota(jnp.int32, shape, 1)
        same = (a // SLOT == b // 16) & (lax.rem(b, 16) // images == s)
        stacked = jnp.concatenate(
            [jnp.broadcast_to(pos[j, 0:1, 0 : blocks * 16], (SLOT, blocks * 16)) for j in range(blocks)], axis=0
        )
        return jnp.where(same & (lax.rem(a, SLOT).astype(F32) == stacked), 1.0, 0.0).astype(BF16)

    for s in range(folds):
        sel_row[s] = pick(pos_row, C, s)
        sel_col[s] = pick(pos_col, R, s)

    for rr in row_peers:
        arrive(proj_r.at[rr], s_proj.at[0], r_proj.at[rr])
    total = proj_r[0]
    for j in range(1, R):
        total = total + proj_r[j]
    residual = cls[r, 0:images, :] + scale[...] * total
    embedding = layer_norm(residual, fgain[...], fshift[...])
    packed = jnp.concatenate([embedding[:, s * wide : (s + 1) * wide] for s in range(folds)], axis=0)
    e_row[c] = packed.astype(BF16)
    e_col[r] = packed.astype(BF16)
    for t, cc in enumerate(col_peers):
        send(e_row.at[c], e_row.at[c], s_emb.at[1, t], r_emb_row.at[c], (r, cc))
    for t, rr in enumerate(row_peers):
        send(e_col.at[r], e_col.at[r], s_emb.at[0, t], r_emb_col.at[r], (rr, c))

    def merged(kept_ref, sel, emb, blocks):
        base = kept_ref[...].reshape(blocks * SLOT, D)
        flat = emb[...].reshape(blocks * 16, wide)
        outs = []
        for s in range(folds):
            moved = jnp.dot(sel[s], flat, preferred_element_type=F32)
            outs.append((base[:, s * wide : (s + 1) * wide].astype(F32) + moved).astype(BF16))
        return jnp.concatenate(outs, axis=1)

    for rr in row_peers:
        arrive(e_col.at[rr], s_cls.at[0], r_emb_col.at[rr])
    for cc in col_peers:
        arrive(e_row.at[cc], s_cls.at[0], r_emb_row.at[cc])
    rows = merged(a_row, sel_row, e_row, C)
    cols = merged(a_col, sel_col, e_col, R)
    inner = lax.dot_general(rows, cols, NT, preferred_element_type=F32)
    base = inner / D + 1.0
    gram = base * base * base
    ga = lax.broadcasted_iota(jnp.int32, gram.shape, 0) - SLOT * c
    gb = lax.broadcasted_iota(jnp.int32, gram.shape, 1) - SLOT * r
    diagonal = (ga == gb) & (ga >= 0) & (ga < rows_dev)
    trace = jnp.sum(jnp.where(diagonal, gram, 0.0))
    product = fold_pieces(jnp.dot(pieces(gram), col_signs[...].astype(BF16), preferred_element_type=F32))
    quad = jnp.sum(row_signs[...] * product, axis=0, keepdims=True) - trace
    quad_c[c] = jnp.broadcast_to(quad, (8, LANES))
    for t, cc in enumerate(col_peers):
        send(quad_c.at[c], quad_c.at[c], s_qc.at[t], r_qc.at[c], (r, cc))
    for j in range(C):
        part[j] = product[j * SLOT : j * SLOT + rows_dev]
    for t, cc in enumerate(col_peers):
        send(part.at[cc], part_r.at[c], s_part.at[t], r_part.at[c], (r, cc))
    part_r[c] = part[c]
    for cc in col_peers:
        arrive(quad_c.at[cc], s_cls.at[0], r_qc.at[cc])
    total = quad_c[0]
    for j in range(1, C):
        total = total + quad_c[j]
    quad_r[r] = total
    for t, rr in enumerate(row_peers):
        send(quad_r.at[r], quad_r.at[r], s_qr.at[t], r_qr.at[r], (rr, c))
    for cc in col_peers:
        arrive(part_r.at[cc], s_cls.at[0], r_part.at[cc])
    summed = part_r[0]
    for j in range(1, C):
        summed = summed + part_r[j]
    proof[...] = (summed * samples ** (-0.5))[:, 0:PERMS]
    for rr in row_peers:
        arrive(quad_r.at[rr], s_cls.at[0], r_qr.at[rr])
    total = quad_r[0]
    for j in range(1, R):
        total = total + quad_r[j]
    stat[...] = (total[0:1, :] / samples)[:, 0:PERMS]
    for copy in sent:
        copy.wait_send()


def per_device(
    R, C, tokens, positions, cached, labels, w_kv, w_query, w_out,
    norm_gain, norm_bias, query_bias, value_bias, layer_scale, final_gain, final_bias,
):
    images, tok, D = tokens.shape
    rows_dev = cached.shape[0]
    HR = HEADS // R
    flat = lambda v: v.reshape(1, D)
    vm = pl.BlockSpec(memory_space=pltpu.VMEM)
    sm = pl.BlockSpec(memory_space=pltpu.SMEM)
    V = pltpu.VMEM
    S = lambda *shape: pltpu.SemaphoreType.DMA(shape)
    wide = max(128, 16 * R, 16 * C)
    scratch = [
        V((images, tok, D), BF16), V((images, 16, D), BF16), S(images + 1),
        V((images, tok, D), BF16), V((R, 8, D), F32),
        V((D, D // R), BF16), V((D, D // R), BF16), V((D, D // R), BF16), V((D, D // R), BF16),
        V((C * SLOT, LANES), F32), V((R * SLOT, LANES), F32),
        V((16 // images, C * SLOT, C * 16), BF16), V((16 // images, R * SLOT, R * 16), BF16),
        V((C, SLOT, D), BF16), V((R, SLOT, D), BF16), V((C, 8, wide), F32), V((R, 8, wide), F32),
        V((R, HR * images, D), F32), V((R, HR * images, D), F32),
        V((R, HR * images, D), F32), V((R, HR * images, D), F32),
        V((R, images, D), F32), V((R, images, D), F32),
        V((C, 16, D * images // 16), BF16), V((R, 16, D * images // 16), BF16),
        V((C, rows_dev, LANES), F32), V((C, rows_dev, LANES), F32),
        V((C, 8, LANES), F32), V((R, 8, LANES), F32),
        S(R), S(R), S(4, C), S(4, C), S(4, max(R, C)), S(C), S(R), S(C), S(R),
        S(R), S(R), S(R), S(R), S(R), S(R), S(2, max(R, C)), S(C), S(R),
        S(C), S(C), S(C), S(C), S(R), S(R),
    ]
    proof, stat = pl.pallas_call(
        functools.partial(kernel_body, R, C, images, tok, D, rows_dev),
        out_shape=(
            jax.ShapeDtypeStruct((rows_dev, PERMS), F32),
            jax.ShapeDtypeStruct((1, PERMS), F32),
        ),
        in_specs=[pl.BlockSpec(memory_space=pltpu.HBM), sm] + [vm] * 12,
        out_specs=(vm, vm),
        scratch_shapes=scratch,
        compiler_params=pltpu.CompilerParams(
            collective_id=0, has_side_effects=True, vmem_limit_bytes=48 * 1024 * 1024
        ),
    )(
        tokens, positions, cached, w_query, w_kv, w_out,
        flat(norm_gain), flat(norm_bias), flat(query_bias), flat(value_bias), flat(layer_scale),
        flat(final_gain), flat(final_bias), labels,
    )
    return proof, stat.reshape(PERMS)


def solution(mesh):
    placed = (
        P(("row", "col"), None, None),
        P(("row", "col")),
        P(("row", "col"), None),
        P(),
        P("col", "row"),
        P("col", "row"),
        P("row", "col"),
        P(), P(), P(), P(), P(), P(), P(),
    )
    return jax.shard_map(
        functools.partial(per_device, mesh.shape["row"], mesh.shape["col"]),
        mesh=mesh,
        in_specs=placed,
        out_specs=(P(("row", "col"), None), P()),
        check_vma=False,
    )
```

```python
import functools
import jax
import jax.numpy as jnp
from jax import lax
from jax.experimental import pallas as pl
from jax.experimental.pallas import tpu as pltpu
from jax.sharding import PartitionSpec as P

HEADS = 16
PERMS = 240
LANES = 256
SLOT = 32
F32 = jnp.float32
BF16 = jnp.bfloat16
NT = (((1,), (1,)), ((), ()))


def layer_norm(values, gain, shift):
    center = values - jnp.mean(values, axis=-1, keepdims=True)
    spread = jnp.mean(center * center, axis=-1, keepdims=True)
    return center * lax.rsqrt(spread + 1e-06) * gain + shift


def pieces(values, count=3):
    parts = []
    for _ in range(count):
        part = values.astype(BF16)
        parts.append(part)
        values = values - part.astype(F32)
    return jnp.concatenate(parts, axis=0)


def fold_pieces(values, count=3):
    rows = values.shape[0] // count
    total = values[:rows]
    for step in range(1, count):
        total = total + values[step * rows : (step + 1) * rows]
    return total


def kernel_body(
    R, C, images, tok, D, rows_dev,
    tokens_hbm, positions, cached, wq, wkv, wo,
    gain, shift, qbias, vbias, scale, fgain, fshift, labels,
    proof, stat,
    tokens, heads16, d_tok, normed, cls, wq_g, wk_g, wv_g, wo_g, row_signs, col_signs, sel_row, sel_col,
    a_row, a_col, pos_row, pos_col, fold_s, fold_r, pool_s, pool_b, pool_r, proj_s, proj_r,
    e_row, e_col, part, part_r, quad_c, quad_r,
    s_cls, r_cls, s_w, r_w, s_cach, r_cach_row, r_cach_col, r_pos_row, r_pos_col,
    s_fold, r_fold, s_pool, r_pool, s_proj, r_proj, s_emb, r_emb_row, r_emb_col,
    s_part, r_part, s_qc, r_qc, s_qr, r_qr,
):
    r = lax.axis_index("row")
    c = lax.axis_index("col")
    HR = HEADS // R
    head = D // HEADS
    half = C // 2
    core = lax.rem(c, 2)
    sib = c + 1 - 2 * core
    row_peers = [lax.rem(r + t, R) for t in range(1, R)]
    col_peers = [lax.rem(c + t, C) for t in range(1, C)]
    chip_peers = [core + 2 * lax.rem(c // 2 + t, half) for t in range(1, half)]
    sent = []

    def send(src, dst, ssem, rsem, dev):
        copy = pltpu.make_async_remote_copy(
            src_ref=src, dst_ref=dst, send_sem=ssem, recv_sem=rsem,
            device_id=dev, device_id_type=pl.DeviceIdType.MESH,
        )
        copy.start()
        sent.append(copy)

    def arrive(dst, ssem, rsem):
        pltpu.make_async_remote_copy(
            src_ref=dst, dst_ref=dst, send_sem=ssem, recv_sem=rsem,
            device_id=(r, sib), device_id_type=pl.DeviceIdType.MESH,
        ).wait_recv()

    head_copy = pltpu.make_async_copy(tokens_hbm.at[:, pl.ds(0, 16), :], heads16, d_tok.at[images])
    head_copy.start()
    loads = [pltpu.make_async_copy(tokens_hbm.at[i], tokens.at[i], d_tok.at[i]) for i in range(images)]
    for load in loads:
        load.start()
    barrier = pltpu.get_barrier_semaphore()
    for rr in row_peers:
        pl.semaphore_signal(barrier, inc=1, device_id=(rr, c), device_id_type=pl.DeviceIdType.MESH)
    for cc in col_peers:
        pl.semaphore_signal(barrier, inc=1, device_id=(r, cc), device_id_type=pl.DeviceIdType.MESH)

    wrows = D // C

    def wslot(ref, index):
        return ref.at[pl.ds(pl.multiple_of(index * wrows, wrows), wrows)]

    head_copy.wait()
    cls[r] = jnp.zeros(cls.shape[1:], F32)
    for i in range(images):
        cls[r, i : i + 1, :] = heads16[i].astype(F32)[0:1]
    weights = (wq_g, wk_g, wv_g, wo_g)
    both = [wkv[:, s * head : (s + 1) * head] for s in range(2 * HR)]
    wslot(wq_g, c)[...] = wq[...]
    wslot(wk_g, c)[...] = jnp.concatenate(both[0::2], axis=1)
    wslot(wv_g, c)[...] = jnp.concatenate(both[1::2], axis=1)
    wslot(wo_g, c)[...] = wo[...].astype(F32).T.astype(BF16)
    pl.semaphore_wait(barrier, R - 1 + C - 1)

    for t, rr in enumerate(row_peers):
        send(cls.at[r], cls.at[r], s_cls.at[t], r_cls.at[r], (rr, c))
    for w, full in enumerate(weights):
        for t, cc in enumerate(chip_peers + [sib]):
            send(wslot(full, c), wslot(full, c), s_w.at[w, t], r_w.at[w, c], (r, cc))
    first_row = (r * C + c) * rows_dev
    local = [(positions[i] - first_row).astype(F32) for i in range(images)]
    sub = lax.broadcasted_iota(jnp.int32, (rows_dev, 1), 0).astype(F32)
    hit = jnp.zeros((rows_dev, 1), F32)
    for value in local:
        hit = jnp.where(sub == value, 1.0, hit)
    kept = cached[...].astype(F32) * (1.0 - hit)
    kept = jnp.concatenate([kept, jnp.zeros((SLOT - rows_dev, D), F32)], axis=0).astype(BF16)
    a_row[c] = kept
    a_col[r] = kept
    lane4 = lax.rem(lax.broadcasted_iota(jnp.int32, pos_row.shape[1:], 1), images)
    tile = jnp.zeros(pos_row.shape[1:], F32)
    for i in range(images):
        tile = jnp.where(lane4 == i, local[i], tile)
    pos_row[c] = tile
    pos_col[r] = tile

    def forward(w):
        full = weights[w]
        for t, cc in enumerate(chip_peers):
            arrive(wslot(full, cc), s_w.at[w, 0], r_w.at[w, cc])
            send(wslot(full, cc), wslot(full, cc), s_w.at[w, half + t], r_w.at[w, cc], (r, sib))

    def complete(w):
        full = weights[w]
        arrive(wslot(full, sib), s_w.at[w, 0], r_w.at[w, sib])
        for cc in chip_peers:
            other = cc + 1 - 2 * core
            arrive(wslot(full, other), s_w.at[w, 0], r_w.at[w, other])

    def share():
        for t, rr in enumerate(row_peers):
            send(a_col.at[r], a_col.at[r], s_cach.at[0, t], r_cach_col.at[r], (rr, c))
            send(pos_col.at[r], pos_col.at[r], s_cach.at[1, t], r_pos_col.at[r], (rr, c))
        for t, cc in enumerate(chip_peers + [sib]):
            send(a_row.at[c], a_row.at[c], s_cach.at[2, t], r_cach_row.at[c], (r, cc))
        for t, cc in enumerate(col_peers):
            send(pos_row.at[c], pos_row.at[c], s_cach.at[3, t], r_pos_row.at[c], (r, cc))

    def share_on():
        for t, cc in enumerate(chip_peers):
            arrive(a_row.at[cc], s_cls.at[0], r_cach_row.at[cc])
            send(a_row.at[cc], a_row.at[cc], s_cach.at[2, half + t], r_cach_row.at[cc], (r, sib))

    def norm_image(i):
        loads[i].wait()

        @pl.loop(0, tok // 32, unroll=2)
        def _(j):
            at = pl.ds(pl.multiple_of(j * 32, 32), 32)
            normed[i, at, :] = layer_norm(tokens[i, at, :].astype(F32), gain[...], shift[...]).astype(BF16)
        last = (tok // 32) * 32
        if last < tok:
            normed[i, last:tok, :] = layer_norm(
                tokens[i, last:tok, :].astype(F32), gain[...], shift[...]
            ).astype(BF16)

    for i in range(images // 2):
        norm_image(i)
    forward(0)
    for i in range(images // 2, images):
        norm_image(i)

    for rr in row_peers:
        arrive(cls.at[rr], s_cls.at[0], r_cls.at[rr])
    group = jnp.concatenate([cls[j, 0:images, :] for j in range(R)], axis=0)
    normed0 = layer_norm(group, gain[...], shift[...]).astype(BF16)

    def own_part(ref):
        size = D // R
        part = ref[:, 0:size]
        for j in range(1, R):
            part = jnp.where(r == j, ref[:, j * size : (j + 1) * size], part)
        return part

    complete(0)
    query = jnp.dot(normed0, wq_g[...], preferred_element_type=F32) + own_part(qbias)
    query = query * head ** (-0.5)
    count = R * images
    of_head = lax.broadcasted_iota(jnp.int32, query.shape, 1) // head
    spread = jnp.concatenate([jnp.where(of_head == h, query, 0.0) for h in range(HR)], axis=0)
    spread = pieces(spread)
    forward(1)
    complete(1)
    folded = fold_pieces(lax.dot_general(spread, wk_g[...], NT, preferred_element_type=F32))
    for h in range(HR):
        for j in range(R):
            at = h * count + j * images
            fold_s[j, h * images : (h + 1) * images, :] = folded[at : at + images]
    for t, rr in enumerate(row_peers):
        send(fold_s.at[rr], fold_r.at[r], s_fold.at[t], r_fold.at[r], (rr, c))
    fold_r[r] = fold_s[r]
    forward(2)
    share()
    samples = rows_dev * R * C
    step = min(samples, 768)

    def chosen(count, first):
        a = lax.broadcasted_iota(jnp.int32, (count * SLOT, step), 0)
        m = lax.broadcasted_iota(jnp.int32, (count * SLOT, step), 1)
        return a // SLOT, lax.rem(a, SLOT), m + first

    row_signs[...] = jnp.zeros(row_signs.shape, F32)
    col_signs[...] = jnp.zeros(col_signs.shape, F32)

    @pl.loop(0, samples // step)
    def _(turn):
        first = pl.multiple_of(turn * step, step)
        perm = lax.broadcasted_iota(jnp.int32, (LANES, step), 0)
        word = jnp.zeros((LANES, step), jnp.int32)
        for w in range(labels.shape[0]):
            word = jnp.where(perm // 30 == w, labels[w : w + 1, pl.ds(first, step)], word)
        bits = jnp.bitwise_and(jnp.right_shift(word, lax.rem(perm, 30)), 1)
        signs = jnp.where(perm < PERMS, 2 * bits - 1, 0).astype(F32).astype(BF16)
        block, inside, m = chosen(C, first)
        one = (m == (r * C + block) * rows_dev + inside) & (inside < rows_dev)
        one = jnp.where(one, 1.0, 0.0).astype(BF16)
        row_signs[...] += lax.dot_general(one, signs, NT, preferred_element_type=F32)
        block, inside, m = chosen(R, first)
        one = (m == (block * C + c) * rows_dev + inside) & (inside < rows_dev)
        one = jnp.where(one, 1.0, 0.0).astype(BF16)
        col_signs[...] += lax.dot_general(one, signs, NT, preferred_element_type=F32)

    for rr in row_peers:
        arrive(fold_r.at[rr], s_fold.at[0], r_fold.at[rr])
    forward(3)

    scores = []
    for i in range(images):
        mine = jnp.concatenate(
            [fold_r[j, h * images + i : h * images + i + 1, :] for j in range(R) for h in range(HR)], axis=0
        )
        scores.append(
            fold_pieces(lax.dot_general(pieces(mine), normed[i], NT, preferred_element_type=F32))
        )
    scores = jnp.concatenate(scores, axis=0)
    expo = jnp.exp(scores - jnp.max(scores, axis=-1, keepdims=True))
    attend = expo / jnp.sum(expo, axis=-1, keepdims=True)
    for i in range(images):
        weight = pieces(attend[i * HEADS : (i + 1) * HEADS])
        pooled = fold_pieces(jnp.dot(weight, normed[i], preferred_element_type=F32))
        for j in range(R):
            for h in range(HR):
                at = h * images + i
                pool_s[j, at : at + 1, :] = pooled[j * HR + h : j * HR + h + 1]
    pool_b[...] = pool_s[...].astype(BF16)
    for t, rr in enumerate(row_peers):
        send(pool_b.at[rr], pool_r.at[r], s_pool.at[t], r_pool.at[r], (rr, c))
    pool_r[r] = pool_b[r]
    complete(2)
    complete(3)
    share_on()
    for rr in row_peers:
        arrive(pool_r.at[rr], s_pool.at[0], r_pool.at[rr])

    blocks = [pool_r[j].astype(F32) for j in range(R)]
    mine = jnp.concatenate(
        [blocks[j][h * images : (h + 1) * images, :] for h in range(HR) for j in range(R)], axis=0
    ).astype(BF16)
    got = jnp.dot(mine, wv_g[...], preferred_element_type=F32)
    mixed = jnp.where(of_head == 0, got[0:count], 0.0)
    for h in range(1, HR):
        mixed = jnp.where(of_head == h, got[h * count : (h + 1) * count], mixed)
    mixed = (mixed + own_part(vbias)).astype(BF16)
    projected = lax.dot_general(mixed, wo_g[...], NT, preferred_element_type=F32)
    for j in range(R):
        proj_s[j] = projected[j * images : (j + 1) * images]
    for t, rr in enumerate(row_peers):
        send(proj_s.at[rr], proj_r.at[r], s_proj.at[t], r_proj.at[r], (rr, c))
    proj_r[r] = proj_s[r]

    folds = 16 // images
    wide = D // folds
    for rr in row_peers:
        arrive(a_col.at[rr], s_cls.at[0], r_cach_col.at[rr])
        arrive(pos_col.at[rr], s_cls.at[0], r_pos_col.at[rr])
    for cc in col_peers:
        arrive(pos_row.at[cc], s_cls.at[0], r_pos_row.at[cc])
    for cc in [sib] + [cc + 1 - 2 * core for cc in chip_peers]:
        arrive(a_row.at[cc], s_cls.at[0], r_cach_row.at[cc])

    def pick(pos, blocks, s):
        shape = (blocks * SLOT, blocks * 16)
        a = lax.broadcasted_iota(jnp.int32, shape, 0)
        b = lax.broadcasted_iota(jnp.int32, shape, 1)
        same = (a // SLOT == b // 16) & (lax.rem(b, 16) // images == s)
        stacked = jnp.concatenate(
            [jnp.broadcast_to(pos[j, 0:1, 0 : blocks * 16], (SLOT, blocks * 16)) for j in range(blocks)], axis=0
        )
        return jnp.where(same & (lax.rem(a, SLOT).astype(F32) == stacked), 1.0, 0.0).astype(BF16)

    for s in range(folds):
        sel_row[s] = pick(pos_row, C, s)
        sel_col[s] = pick(pos_col, R, s)

    for rr in row_peers:
        arrive(proj_r.at[rr], s_proj.at[0], r_proj.at[rr])
    total = proj_r[0]
    for j in range(1, R):
        total = total + proj_r[j]
    residual = cls[r, 0:images, :] + scale[...] * total
    embedding = layer_norm(residual, fgain[...], fshift[...])
    packed = jnp.concatenate([embedding[:, s * wide : (s + 1) * wide] for s in range(folds)], axis=0)
    e_row[c] = packed.astype(BF16)
    e_col[r] = packed.astype(BF16)
    for t, cc in enumerate(col_peers):
        send(e_row.at[c], e_row.at[c], s_emb.at[1, t], r_emb_row.at[c], (r, cc))
    for t, rr in enumerate(row_peers):
        send(e_col.at[r], e_col.at[r], s_emb.at[0, t], r_emb_col.at[r], (rr, c))

    def merged(kept_ref, sel, emb, blocks):
        base = kept_ref[...].reshape(blocks * SLOT, D)
        flat = emb[...].reshape(blocks * 16, wide)
        outs = []
        for s in range(folds):
            moved = jnp.dot(sel[s], flat, preferred_element_type=F32)
            outs.append((base[:, s * wide : (s + 1) * wide].astype(F32) + moved).astype(BF16))
        return jnp.concatenate(outs, axis=1)

    for rr in row_peers:
        arrive(e_col.at[rr], s_cls.at[0], r_emb_col.at[rr])
    for cc in col_peers:
        arrive(e_row.at[cc], s_cls.at[0], r_emb_row.at[cc])
    rows = merged(a_row, sel_row, e_row, C)
    cols = merged(a_col, sel_col, e_col, R)
    inner = lax.dot_general(rows, cols, NT, preferred_element_type=F32)
    base = inner / D + 1.0
    gram = base * base * base
    ga = lax.broadcasted_iota(jnp.int32, gram.shape, 0) - SLOT * c
    gb = lax.broadcasted_iota(jnp.int32, gram.shape, 1) - SLOT * r
    diagonal = (ga == gb) & (ga >= 0) & (ga < rows_dev)
    trace = jnp.sum(jnp.where(diagonal, gram, 0.0))
    product = fold_pieces(jnp.dot(pieces(gram), col_signs[...].astype(BF16), preferred_element_type=F32))
    quad = jnp.sum(row_signs[...] * product, axis=0, keepdims=True) - trace
    quad_c[c] = jnp.broadcast_to(quad, (8, LANES))
    for t, cc in enumerate(col_peers):
        send(quad_c.at[c], quad_c.at[c], s_qc.at[t], r_qc.at[c], (r, cc))
    for j in range(C):
        part[j] = product[j * SLOT : j * SLOT + rows_dev]
    for t, cc in enumerate(col_peers):
        send(part.at[cc], part_r.at[c], s_part.at[t], r_part.at[c], (r, cc))
    part_r[c] = part[c]
    for cc in col_peers:
        arrive(quad_c.at[cc], s_cls.at[0], r_qc.at[cc])
    total = quad_c[0]
    for j in range(1, C):
        total = total + quad_c[j]
    quad_r[r] = total
    for t, rr in enumerate(row_peers):
        send(quad_r.at[r], quad_r.at[r], s_qr.at[t], r_qr.at[r], (rr, c))
    for cc in col_peers:
        arrive(part_r.at[cc], s_cls.at[0], r_part.at[cc])
    summed = part_r[0]
    for j in range(1, C):
        summed = summed + part_r[j]
    proof[...] = (summed * samples ** (-0.5))[:, 0:PERMS]
    for rr in row_peers:
        arrive(quad_r.at[rr], s_cls.at[0], r_qr.at[rr])
    total = quad_r[0]
    for j in range(1, R):
        total = total + quad_r[j]
    stat[...] = (total[0:1, :] / samples)[:, 0:PERMS]
    for copy in sent:
        copy.wait_send()


def per_device(
    R, C, tokens, positions, cached, labels, w_kv, w_query, w_out,
    norm_gain, norm_bias, query_bias, value_bias, layer_scale, final_gain, final_bias,
):
    images, tok, D = tokens.shape
    rows_dev = cached.shape[0]
    HR = HEADS // R
    flat = lambda v: v.reshape(1, D)
    vm = pl.BlockSpec(memory_space=pltpu.VMEM)
    sm = pl.BlockSpec(memory_space=pltpu.SMEM)
    V = pltpu.VMEM
    S = lambda *shape: pltpu.SemaphoreType.DMA(shape)
    wide = max(128, 16 * R, 16 * C)
    scratch = [
        V((images, tok, D), BF16), V((images, 16, D), BF16), S(images + 1),
        V((images, tok, D), BF16), V((R, 8, D), F32),
        V((D, D // R), BF16), V((D, D // R), BF16), V((D, D // R), BF16), V((D, D // R), BF16),
        V((C * SLOT, LANES), F32), V((R * SLOT, LANES), F32),
        V((16 // images, C * SLOT, C * 16), BF16), V((16 // images, R * SLOT, R * 16), BF16),
        V((C, SLOT, D), BF16), V((R, SLOT, D), BF16), V((C, 8, wide), F32), V((R, 8, wide), F32),
        V((R, HR * images, D), F32), V((R, HR * images, D), F32), V((R, HR * images, D), F32),
        V((R, HR * images, D), BF16), V((R, HR * images, D), BF16),
        V((R, images, D), F32), V((R, images, D), F32),
        V((C, 16, D * images // 16), BF16), V((R, 16, D * images // 16), BF16),
        V((C, rows_dev, LANES), F32), V((C, rows_dev, LANES), F32),
        V((C, 8, LANES), F32), V((R, 8, LANES), F32),
        S(R), S(R), S(4, C), S(4, C), S(4, max(R, C)), S(C), S(R), S(C), S(R),
        S(R), S(R), S(R), S(R), S(R), S(R), S(2, max(R, C)), S(C), S(R),
        S(C), S(C), S(C), S(C), S(R), S(R),
    ]
    proof, stat = pl.pallas_call(
        functools.partial(kernel_body, R, C, images, tok, D, rows_dev),
        out_shape=(
            jax.ShapeDtypeStruct((rows_dev, PERMS), F32),
            jax.ShapeDtypeStruct((1, PERMS), F32),
        ),
        in_specs=[pl.BlockSpec(memory_space=pltpu.HBM), sm] + [vm] * 12,
        out_specs=(vm, vm),
        scratch_shapes=scratch,
        compiler_params=pltpu.CompilerParams(
            collective_id=0, has_side_effects=True, vmem_limit_bytes=48 * 1024 * 1024
        ),
    )(
        tokens, positions, cached, w_query, w_kv, w_out,
        flat(norm_gain), flat(norm_bias), flat(query_bias), flat(value_bias), flat(layer_scale),
        flat(final_gain), flat(final_bias), labels,
    )
    return proof, stat.reshape(PERMS)


def solution(mesh):
    placed = (
        P(("row", "col"), None, None),
        P(("row", "col")),
        P(("row", "col"), None),
        P(),
        P("col", "row"),
        P("col", "row"),
        P("row", "col"),
        P(), P(), P(), P(), P(), P(), P(),
    )
    return jax.shard_map(
        functools.partial(per_device, mesh.shape["row"], mesh.shape["col"]),
        mesh=mesh,
        in_specs=placed,
        out_specs=(P(("row", "col"), None), P()),
        check_vma=False,
    )
```
